128 devices in a mesh: seq: 32 (over z, y_lo, x), head: 4 (over y_hi, core).
Axes of the slice: x: 4, y: 4 (y_hi: 2, y_lo: 2; y = y_hi * 2 + y_lo), z: 4, core: 2. Of those that a mesh axis runs over, the one named last changes fastest.
Arguments:
- queries: bfloat16 [1024, 3584], P('seq', 'head'), may hold values from -40 to 40
- keys: bfloat16 [32768, 512], P('seq', 'head'), may hold values from -4 to 4
- values: bfloat16 [32768, 512], P('seq', 'head'), may hold values from -6 to 6
- hidden_in: bfloat16 [1024, 3584], P('seq'), may hold values from -6 to 6
- out_grad: bfloat16 [1024, 3584], P('seq'), may hold values from -24 to 24
- w_out: bfloat16 [3584, 3584], P('head'), may hold values from -0.09375 to 0.09375
- q_left: bfloat16 [64, 3584], replicated, may hold values from -0.0234375 to 0.0234375
- q_right: bfloat16 [64, 3584], P(None, 'head'), may hold values from -0.09375 to 0.09375
- o_left: bfloat16 [64, 3584], P(None, 'head'), may hold values from -0.375 to 0.375
- o_right: bfloat16 [64, 3584], replicated, may hold values from -0.01171875 to 0.01171875
- positions: int32 [32, 1024], replicated, may hold values from 0 to 32767, as said below
- doc_ids: int32 [32768], replicated, may hold values from 0 to 31, never falling along the last dimension, each value on 1 to 4096 neighbouring positions
Outputs:
- query_grad: bfloat16 [1024, 3584], P('seq', 'head')
- q_docs: float32 [32, 4096], P('seq', 'head')
- o_docs: float32 [32, 4096], P('seq', 'head')
The draws below stay inside these ranges and needn't reach their ends.
Inputs may be any that keep to these rules, and one draw needn't show every extreme that they name: Each row is 16 stripes: runs of 64 consecutive positions, ascending within the run, each starting at a multiple of 64; every position 0 to 32767 appears once in all.
All inputs are finite; a program needn't handle non-finite values.
Results may differ from the reference program's by a relative error of at most 0.011.
Values may be sent and summed in bfloat16 or wider, within the bound.
No kernel may reach another device: no remote copies, remote signals or barrier semaphores. Data moves between devices by JAX's collectives and lax.ppermute only.
A program may use at most 64 MiB of HBM per device.

```python
import math
import jax
import jax.numpy as jnp
import numpy as np
from jax import lax

D = 3584
HEADS = 28
KV_HEADS = 4
HD = 128
R = 64
STRIPE = 64
KV_DEV = 1024
Q_DEV = 32
SEQ = 32768
QTOK = 1024
DOCS = 32
DOC_MOST = 4096


def draw_queries(key, part):
    key = jax.random.fold_in(key, 3)
    row_count = Q_DEV * (SEQ // KV_DEV)
    sample = jnp.clip(jax.random.normal(key, (row_count, HEADS * HD)), -4.0, 4.0)
    return sample.astype(jnp.bfloat16)


def draw_keys(key, part):
    key = jax.random.fold_in(key, 5)
    sample = jnp.clip(jax.random.normal(key, (SEQ, KV_HEADS * HD)), -4.0, 4.0)
    return sample.astype(jnp.bfloat16)


def draw_positions(key, part):
    key = jax.random.fold_in(key, 7)
    stripe_count = SEQ // STRIPE
    order = jax.random.permutation(key, stripe_count)
    spread = order[:, None] * STRIPE + jnp.arange(STRIPE)[None, :]
    return spread.reshape(SEQ // KV_DEV, KV_DEV).astype(jnp.int32)


def levels(key, shape, cuts, least, high):
    def one(position, parts):
        draws = jax.random.uniform(jax.random.fold_in(jax.random.fold_in(key, 6), position), (parts,), jnp.float32, least / len(cuts), high / len(cuts))
        return jnp.repeat(jnp.exp(draws), shape[position] // parts).reshape((-1,) + (1,) * (len(shape) - position - 1))

    level = one(*cuts[0])
    for cut in cuts[1:]:
        level = level * one(*cut)
    return level


def profile(amount, total, bound, slope):
    loads = [(1 << 20) // math.isqrt(standing ** slope) + 1 for standing in range(2, amount + 1)]
    spare, holding = total - bound - (amount - 1), [1] * (amount - 1)
    while spare > 0:
        free = [i for i in range(amount - 1) if holding[i] < bound]
        mass, budget = sum([loads[i] for i in free]), spare
        for i in free:
            more = min(bound - holding[i], max(1, budget * loads[i] // mass), spare)
            holding[i] = holding[i] + more
            spare = spare - more
    return np.array([bound] + holding)


def uneven(key, amount, total, most, lean):
    if amount == 2:
        one = jax.random.randint(key, (), max(1, total - most), min(most, total - 1) + 1)
        return jnp.stack([one, total - one])
    lengths = jnp.asarray(profile(amount, total, most, lean), jnp.int32)
    twos = (amount - 1) // 2
    giver, sink = lengths[1:1 + 2 * twos:2], lengths[2:2 + 2 * twos:2]
    slack = jnp.minimum(giver - 1, most - sink)
    shifted = jax.random.randint(jax.random.fold_in(key, 1), (twos,), 0, 1 << 20) % (slack + 1)
    lengths = lengths.at[1:1 + 2 * twos:2].set(giver - shifted).at[2:2 + 2 * twos:2].set(sink + shifted)
    return lengths[jax.random.permutation(jax.random.fold_in(key, 2), amount)]


def noise(key, dims, width, reach, shards=(), kind=jnp.bfloat16):
    array = jax.random.normal(key, dims, jnp.float32) * width
    if len(shards) > 0:
        array = levels(key, dims, shards, -0.22, 0.18) * array
    return jnp.clip(array, min=-reach, max=reach).astype(kind)


def setup_inputs(seed: int = 0) -> dict:
    seeds = jax.random.split(jax.random.key(seed), 13)
    queries = draw_queries(jax.random.fold_in(seeds[12], 71), 0)
    keys = draw_keys(jax.random.fold_in(seeds[12], 71), 0)
    values = noise(seeds[2], (SEQ, KV_HEADS * HD), 1.0, 6.0, ((0, 32), (1, 4)))
    hidden_in = noise(seeds[3], (QTOK, D), 1.0, 6.0, ((0, 32),))
    out_grad = noise(seeds[4], (QTOK, D), 4.0, 24.0, ((0, 32),))
    w_out = noise(seeds[5], (D, D), D ** -0.5, 0.09375, ((0, 4),))
    q_left = noise(seeds[6], (R, D), (16 * D) ** -0.5, 0.0234375)
    q_right = noise(seeds[7], (R, D), D ** -0.5, 0.09375, ((1, 4),))
    o_left = noise(seeds[8], (R, D), (D // 16) ** -0.5, 0.375, ((1, 4),))
    o_right = noise(seeds[9], (R, D), (64 * D) ** -0.5, 0.01171875)
    positions = draw_positions(jax.random.fold_in(seeds[12], 71), 0)
    doc_ids = jnp.searchsorted(jnp.cumsum(uneven(seeds[11], DOCS, SEQ, DOC_MOST, 1)), jnp.arange(SEQ), side="right").astype(jnp.int32)
    return {"queries": queries, "keys": keys, "values": values, "hidden_in": hidden_in, "out_grad": out_grad, "w_out": w_out, "q_left": q_left, "q_right": q_right, "o_left": o_left, "o_right": o_right, "positions": positions, "doc_ids": doc_ids}


NEG_BIG = -1e+30
ROPE_BASE = 10000000.0

def reference(queries, keys, values, hidden_in, out_grad, w_out, q_left, q_right, o_left, o_right, positions, doc_ids):
    flat_pos = positions.reshape(-1)
    key_doc = doc_ids[flat_pos]
    query_range = jnp.arange(QTOK, dtype=jnp.int32)
    query_index = query_range // Q_DEV * KV_DEV + query_range % Q_DEV
    query_pos = flat_pos[query_index]
    query_doc = key_doc[query_index]
    allowed = (flat_pos[None, :] <= query_pos[:, None]) & (key_doc[None, :] == query_doc[:, None])
    attn_grad = jnp.dot(out_grad, w_out.T, preferred_element_type=jnp.float32).astype(jnp.bfloat16)
    group = HEADS // KV_HEADS
    score_scale = 1.0 / math.sqrt(HD)

    def one_head(head):
        head = head.astype(jnp.int32)
        query_head = lax.dynamic_slice_in_dim(queries, head * HD, HD, axis=1)
        grad_head = lax.dynamic_slice_in_dim(attn_grad, head * HD, HD, axis=1)
        kv_start = (head // group * HD).astype(jnp.int32)
        key_head = lax.dynamic_slice_in_dim(keys, kv_start, HD, axis=1)
        value_head = lax.dynamic_slice_in_dim(values, kv_start, HD, axis=1)
        scores = jnp.dot(query_head, key_head.T, preferred_element_type=jnp.float32) * score_scale
        scores = jnp.where(allowed, scores, NEG_BIG)
        row_max = lax.optimization_barrier(jnp.max(scores, axis=-1))
        weights = jnp.where(allowed, jnp.exp(scores - row_max[:, None]), 0.0)
        log_total = row_max + jnp.log(lax.optimization_barrier(jnp.sum(weights, axis=-1)))
        probs = jnp.where(allowed, jnp.exp(scores - log_total[:, None]), 0.0).astype(jnp.bfloat16)
        out_head = jnp.dot(probs, value_head, preferred_element_type=jnp.float32)
        prob_grad = jnp.dot(grad_head, value_head.T, preferred_element_type=jnp.float32)
        weighted = (probs * prob_grad).astype(jnp.bfloat16)
        grad_sum = jnp.dot(weighted, key_head, preferred_element_type=jnp.float32)
        key_sum = jnp.dot(probs, key_head, preferred_element_type=jnp.float32)
        delta_row = lax.optimization_barrier(jnp.sum(grad_head.astype(jnp.float32) * out_head, axis=-1))
        raw_grad = (grad_sum - delta_row[:, None] * key_sum) * score_scale
        return (out_head, raw_grad)
    out_heads, grad_heads = lax.map(one_head, jnp.arange(HEADS, dtype=jnp.int32))
    half_dim = HD // 2
    inverse_freq = ROPE_BASE ** (-(jnp.arange(half_dim, dtype=jnp.float32) * 2.0) / HD)
    angles = query_pos.astype(jnp.float32)[:, None] * inverse_freq[None, :]
    cosine = jnp.cos(angles)[None, :, :]
    sine_part = jnp.sin(angles)[None, :, :]
    first_half = grad_heads[..., :half_dim]
    second_half = grad_heads[..., half_dim:]
    rotated_back = jnp.concatenate([first_half * cosine + second_half * sine_part, second_half * cosine - first_half * sine_part], axis=-1)
    query_grad = jnp.transpose(rotated_back, (1, 0, 2)).reshape(QTOK, D).astype(jnp.bfloat16)
    attn_out = jnp.transpose(out_heads, (1, 0, 2)).reshape(QTOK, D).astype(jnp.bfloat16)
    onehot = (query_doc[:, None] == jnp.arange(DOCS, dtype=jnp.int32)[None, :]).astype(jnp.float32)

    def per_doc(left_side, right_side):
        outer = (left_side[:, :, None] * right_side[:, None, :]).reshape(QTOK, R * R)
        return jnp.dot(onehot.T, outer, precision=lax.Precision.HIGHEST)
    q_docs = per_doc(jnp.dot(hidden_in, q_left.T, preferred_element_type=jnp.float32), jnp.dot(query_grad, q_right.T, preferred_element_type=jnp.float32))
    o_docs = per_doc(jnp.dot(attn_out, o_left.T, preferred_element_type=jnp.float32), jnp.dot(out_grad, o_right.T, preferred_element_type=jnp.float32))
    return (query_grad, q_docs, o_docs)
```

```python
import functools
import math

import jax
import jax.numpy as jnp
from jax import lax
from jax.experimental import pallas as pl
from jax.experimental.pallas import tpu as pltpu
from jax.sharding import Mesh
from jax.sharding import PartitionSpec as P

ROPE_BASE = 10000000.0
MASKED = -1e30
EMPTY = -1e20
STRIPE = 64
CHUNK = 4
KV_LANES = 256
STAT = 8
F32 = jnp.float32
BF16 = jnp.bfloat16

SEQ_AXES = ("z", "y", "x")
FAR = ("z", "y")
VMEM = pl.BlockSpec(memory_space=pltpu.VMEM)
SMEM = pl.BlockSpec(memory_space=pltpu.SMEM)
LIMIT = 48 * 1024 * 1024


def dot_t(left, right, **kw):
    return lax.dot_general(
        left, right, (((1,), (1,)), ((), ())), preferred_element_type=F32, **kw
    )


def shifted(block, axis, distance):
    size = lax.axis_size(axis)
    return lax.ppermute(block, axis, [(i, (i + distance) % size) for i in range(size)])


def spread(block, axes, count):
    return lax.all_to_all(jnp.broadcast_to(block[None], (count,) + block.shape), axes, 0, 0)


def plan_kernel(rows, blocks, index_ref, first_ref, doc_ref, count_ref, list_ref, base_ref, start_ref, first_of):
    x, z_y = index_ref[0], index_ref[1]
    docs = doc_ref[...]
    lane = lax.broadcasted_iota(jnp.int32, (1, 32), 1)
    begin = jnp.zeros((1, 32), F32)
    for doc in range(32):
        below = jnp.sum(jnp.where(docs < doc, 1.0, 0.0).astype(F32))
        begin = begin + jnp.where(lane == doc, below, 0.0)
    row_i = lax.broadcasted_iota(jnp.int32, (rows, 32), 0)
    lane_i = lax.broadcasted_iota(jnp.int32, (rows, 32), 1)

    def one_block(b, _):
        first = first_ref[b * 4 + x, 0]
        line = doc_ref[pl.ds(first // 128, 1), :]
        doc_row = jnp.where(first % 128 == 0, line[:, 0:32], line[:, 64:96])
        doc_col = jnp.sum(jnp.where(row_i == lane_i, doc_row.astype(F32), 0.0), axis=1, keepdims=True)
        start = jnp.sum(jnp.where(doc_col == lane_i.astype(F32), begin, 0.0), axis=1, keepdims=True)
        start_ref[pl.ds(b, 1)] = jnp.broadcast_to(start[None], (1, rows, 128))
        low = jnp.min(start).astype(jnp.int32) // STRIPE * STRIPE
        first_of[b] = first

        def one_stripe(t, n):
            shard = t // 16
            source = z_y * 4 + (x + 4 - jnp.where(shard == 2, 3, jnp.where(shard == 3, 2, shard))) % 4
            base = first_ref[source, t % 16]
            list_ref[b * 64 + n] = t
            base_ref[b * 64 + n] = base
            return n + jnp.where((base >= low) & (base <= first), 1, 0)

        count_ref[b] = lax.fori_loop(0, 64, one_stripe, 0)
        return 0

    lax.fori_loop(0, blocks, one_block, 0)


def attend_kernel(
    heads, count_ref, list_ref, base_ref, first_ref, start_ref, qd_ref, kv0, kv1, kv2, kv3, out_ref, kv_all, kv_now, acc_ref
):
    b = pl.program_id(0)
    rows = qd_ref.shape[1]
    hd = 128
    width = heads * hd

    @pl.when(b == 0)
    def _():
        for j, part in enumerate((kv0, kv1, kv2, kv3)):
            kv_all[j * 1024 : (j + 1) * 1024, :] = part[...]

    q = jnp.concatenate([qd_ref[0, :, h * hd : (h + 1) * hd] for h in range(heads)], axis=0)
    d = jnp.concatenate([qd_ref[0, :, width + h * hd : width + (h + 1) * hd] for h in range(heads)], axis=0)
    first = first_ref[b]
    n = count_ref[b]
    keys = CHUNK * STRIPE
    start = start_ref[0, :, 0:1].astype(jnp.int32)
    here = first + lax.broadcasted_iota(jnp.int32, (rows, 1), 0)
    lane = lax.broadcasted_iota(jnp.int32, (1, keys), 1)
    acc_ref[...] = jnp.zeros_like(acc_ref)
    scale = 1.0 / math.sqrt(hd)

    def chunk(c, carried):
        m, l = carried
        key_pos = lane % STRIPE
        for u in range(CHUNK):
            slot = c * CHUNK + u
            valid = slot < n
            entry = jnp.where(valid, list_ref[b * 64 + jnp.minimum(slot, 63)], 0)
            base = jnp.where(valid, base_ref[b * 64 + jnp.minimum(slot, 63)], 1 << 24)
            kv_now[u * STRIPE : (u + 1) * STRIPE, :] = kv_all[pl.ds(pl.multiple_of(entry * STRIPE, STRIPE), STRIPE), :]
            key_pos = key_pos + jnp.where(lane // STRIPE == u, base, 0)
        bias = jnp.where((key_pos >= start) & (key_pos <= here), 0.0, MASKED).astype(F32)
        bias = jnp.concatenate([bias] * heads, axis=0)
        v, k = kv_now[:, 0:hd], kv_now[:, hd : 2 * hd]
        s = dot_t(q, k) * scale + bias
        dp = dot_t(d, v)
        top = jnp.max(s, axis=1, keepdims=True).astype(BF16).astype(F32)
        m_new = jnp.maximum(m, top)
        p = jnp.exp(s - m_new)
        shrink = jnp.exp(m - m_new)
        l = l * shrink + jnp.sum(p, axis=1, keepdims=True)
        pb = p.astype(BF16)
        w = (pb.astype(F32) * dp).astype(BF16)
        acc_ref[:, 0 : 2 * hd] = acc_ref[:, 0 : 2 * hd] * shrink + jnp.dot(pb, kv_now[...], preferred_element_type=F32)
        acc_ref[:, 2 * hd :] = acc_ref[:, 2 * hd :] * shrink + jnp.dot(w, k, preferred_element_type=F32)
        return m_new, l

    zero = (jnp.full((rows * heads, 1), EMPTY, F32), jnp.zeros((rows * heads, 1), F32))
    m, l = lax.fori_loop(0, (n + CHUNK - 1) // CHUNK, chunk, zero)
    l_high = l.astype(BF16).astype(F32)
    l_low = l - l_high
    stat_lane = lax.broadcasted_iota(jnp.int32, (rows, 128), 1)
    stats = jnp.zeros((rows, 128), F32)
    for h in range(heads):
        part = slice(h * rows, (h + 1) * rows)
        out_ref[0, :, h * 3 * hd : (h + 1) * 3 * hd] = acc_ref[part, :].astype(BF16)
        stats = jnp.where(stat_lane == h, m[part], stats)
        stats = jnp.where(stat_lane == STAT + h, l_high[part], stats)
        stats = jnp.where(stat_lane == 2 * STAT + h, l_low[part], stats)
    out_ref[0, :, heads * 3 * hd :] = stats.astype(BF16)


def combine_kernel(heads, part_ref, d_ref, cos_ref, sin_ref, right_ref, left_ref, grad_ref, tail_ref, out_ref):
    blocks = part_ref.shape[0]
    hd = 128
    stat = heads * 3 * hd
    stats = [part_ref[r, :, stat : stat + 128].astype(F32) for r in range(blocks)]
    tops = [s[:, 0:STAT] for s in stats]
    sums = [s[:, STAT : 2 * STAT] + s[:, 2 * STAT : 3 * STAT] for s in stats]
    top = functools.reduce(jnp.maximum, tops)
    weights = [jnp.exp(t - top) for t in tops]
    total = sum(w * s for w, s in zip(weights, sums))
    total = jnp.where(lax.broadcasted_iota(jnp.int32, total.shape, 1) < heads, total, 1.0)
    weights = [w / total for w in weights]
    scale = 1.0 / math.sqrt(hd)
    cos, sin = cos_ref[...], sin_ref[...]
    for h in range(heads):
        cols = slice(h * hd, (h + 1) * hd)
        whole = sum(
            weights[r][:, h : h + 1] * part_ref[r, :, h * 3 * hd : (h + 1) * 3 * hd].astype(F32)
            for r in range(blocks)
        )
        attn, key_sum, grad_sum = whole[:, 0:hd], whole[:, hd : 2 * hd], whole[:, 2 * hd :]
        delta = jnp.sum(d_ref[:, cols].astype(F32) * attn, axis=1, keepdims=True)
        raw = (grad_sum - delta * key_sum) * scale
        turned = jnp.concatenate([raw[:, hd // 2 :], raw[:, : hd // 2]], axis=1)
        grad_ref[:, cols] = (raw * cos + turned * sin).astype(BF16)
        out_ref[:, cols] = attn.astype(BF16)
    tail_ref[:, 0:64] = dot_t(grad_ref[...], right_ref[...])
    tail_ref[:, 64:128] = dot_t(out_ref[...], left_ref[...])


def docs_kernel(index_ref, head_ref, q_left_ref, o_right_ref, doc_ref, out_ref):
    h = index_ref[2]
    whole = head_ref[0] + head_ref[1] + head_ref[2] + head_ref[3]
    q_right, o_left_all = whole[:, 0:64], whole[:, 64:128]
    o_left = jnp.zeros((whole.shape[0], 16), F32)
    for k in range(4):
        o_left = o_left + jnp.where(h == k, o_left_all[:, 16 * k : 16 * k + 16], 0.0)
    doc = doc_ref[...]
    lane = lax.broadcasted_iota(jnp.int32, (whole.shape[0], 512), 1)
    mine = doc[:, 0:1] == lane // 16

    def terms(left, right):
        tiled = jnp.concatenate([left] * 8, axis=1)
        tiled = jnp.concatenate([tiled] * 4, axis=1)
        return lax.dot_general(
            jnp.where(mine, tiled, 0.0),
            right,
            (((0,), (0,)), ((), ())),
            preferred_element_type=F32,
            precision=lax.Precision.HIGHEST,
        )

    both = jnp.concatenate([terms(q_left_ref[...], q_right), terms(o_left, o_right_ref[...])], axis=1)
    out_ref[...] = both.reshape(out_ref.shape).astype(out_ref.dtype)


def total_kernel(part_ref, q_ref, o_ref):
    total = jnp.sum(part_ref[...].astype(F32), axis=0)
    for k in range(8):
        for side, ref in ((0, q_ref), (64, o_ref)):
            pair = [total[2 * k + j : 2 * k + j + 1, side : side + 64] for j in range(2)]
            ref[:, 128 * k : 128 * k + 128] = jnp.concatenate(pair, axis=1)


def call(kernel, out_shape, in_specs, out_specs, **kw):
    return pl.pallas_call(
        kernel,
        out_shape=out_shape,
        in_specs=in_specs,
        out_specs=out_specs,
        compiler_params=pltpu.CompilerParams(vmem_limit_bytes=LIMIT),
        **kw,
    )


def per_device(
    queries, keys, values, hidden_in, out_grad, w_out, q_left, q_right, o_left, o_right, positions, doc_ids
):
    shape = jax.ShapeDtypeStruct
    rows, width = queries.shape
    hd = keys.shape[1]
    heads = width // hd
    blocks = 8
    z, y, x, head = (lax.axis_index(a) for a in ("z", "y", "x", "head"))
    seq = (z * 2 + y) * 4 + x

    kv = jnp.concatenate([values, keys], axis=1)
    half = kv.shape[0] // 2
    kv_before = shifted(kv, "x", 1)
    kv_after = shifted(kv, "x", -1)
    kv_far = jnp.concatenate(
        [shifted(kv_before[:half], "x", 1), shifted(kv_after[half:], "x", -1)], axis=0
    )

    attn_grad = dot_t(out_grad, w_out).astype(BF16)
    mine = jnp.concatenate([queries, attn_grad], axis=1)
    qd = spread(mine, FAR, blocks)

    firsts = positions.reshape(32, 16, STRIPE)[:, :, 0]
    index = jnp.stack([x, z * 2 + y, head]).astype(jnp.int32)
    count, stripes, bases, starts, block_first = call(
        functools.partial(plan_kernel, rows, blocks),
        (
            shape((blocks,), jnp.int32),
            shape((blocks * 64,), jnp.int32),
            shape((blocks * 64,), jnp.int32),
            shape((blocks, rows, 128), F32),
            shape((blocks,), jnp.int32),
        ),
        [SMEM, SMEM, VMEM],
        (SMEM, SMEM, SMEM, VMEM, SMEM),
    )(index, firsts, doc_ids.reshape(256, 128))

    out_lanes = heads * 3 * hd + 128
    whole = pl.BlockSpec(memory_space=pltpu.VMEM)
    parts = call(
        functools.partial(attend_kernel, heads),
        shape((blocks, rows, out_lanes), BF16),
        [
            SMEM,
            SMEM,
            SMEM,
            SMEM,
            pl.BlockSpec((1, rows, 128), lambda b: (b, 0, 0)),
            pl.BlockSpec((1, rows, 2 * width), lambda b: (b, 0, 0)),
            whole,
            whole,
            whole,
            whole,
        ],
        pl.BlockSpec((1, rows, out_lanes), lambda b: (b, 0, 0)),
        grid=(blocks,),
        scratch_shapes=[
            pltpu.VMEM((4096, 2 * hd), BF16),
            pltpu.VMEM((CHUNK * STRIPE, 2 * hd), BF16),
            pltpu.VMEM((heads * rows, 3 * hd), F32),
        ],
    )(count, stripes, bases, block_first, starts, qd, kv, kv_before, kv_after, kv_far)
    parts = lax.all_to_all(parts, FAR, 0, 0)

    here = lax.dynamic_slice(firsts, (seq, 0), (1, 1))[0, 0]
    angles = (here + jnp.arange(rows, dtype=jnp.int32)).astype(F32)[:, None] * (
        ROPE_BASE ** (-(jnp.arange(hd // 2, dtype=F32) * 2.0) / hd)
    )[None, :]
    cos, sin = jnp.cos(angles), jnp.sin(angles)
    query_grad, tail = call(
        functools.partial(combine_kernel, heads),
        (shape((rows, width), BF16), shape((rows, 128), F32)),
        [VMEM] * 6,
        (VMEM, VMEM),
        scratch_shapes=[pltpu.VMEM((rows, width), BF16)],
    )(
        parts,
        attn_grad,
        jnp.concatenate([cos, cos], axis=1),
        jnp.concatenate([sin, -sin], axis=1),
        q_right,
        o_left,
    )

    q_left_rows = lax.dynamic_slice_in_dim(q_left, head * 16, 16)
    q_side = dot_t(hidden_in, q_left_rows)
    o_side = dot_t(out_grad, o_right)
    doc = jnp.broadcast_to(lax.dynamic_slice_in_dim(doc_ids, here, rows)[:, None], (rows, 128))
    by_doc = call(
        docs_kernel,
        shape((32, 16, 128), BF16),
        [SMEM] + [VMEM] * 4,
        VMEM,
    )(index, lax.all_gather(tail, "head"), q_side, o_side, doc)
    by_doc = lax.all_to_all(by_doc, SEQ_AXES, 0, 0)
    q_docs, o_docs = call(
        total_kernel, (shape((1, 1024), F32), shape((1, 1024), F32)), [VMEM], (VMEM, VMEM)
    )(by_doc)
    return (query_grad, q_docs, o_docs)


def solution(mesh):
    grid = Mesh(mesh.devices.reshape(4, 2, 4, 4), ("z", "y", "x", "head"))
    both, seq, head = P(SEQ_AXES, "head"), P(SEQ_AXES, None), P("head", None)
    placed = (both, both, both, seq, seq, head, P(), P(None, "head"), P(None, "head"), P(), P(), P())
    return jax.shard_map(
        per_device, mesh=grid, in_specs=placed, out_specs=(both, both, both), check_vma=False
    )
```

```python
import functools
import math

import jax
import jax.numpy as jnp
from jax import lax
from jax.experimental import pallas as pl
from jax.experimental.pallas import tpu as pltpu
from jax.sharding import Mesh
from jax.sharding import PartitionSpec as P

ROPE_BASE = 10000000.0
MASKED = -1e30
EMPTY = -1e20
STRIPE = 64
CHUNK = 4
STAT = 8
F32 = jnp.float32
BF16 = jnp.bfloat16

SEQ_AXES = ("z", "y", "x")
FAR = ("z", "y")
VMEM = pl.BlockSpec(memory_space=pltpu.VMEM)
SMEM = pl.BlockSpec(memory_space=pltpu.SMEM)
LIMIT = 12 * 1024 * 1024
ATTEND_LIMIT = 24 * 1024 * 1024


def dot_t(left, right, **kw):
    return lax.dot_general(
        left, right, (((1,), (1,)), ((), ())), preferred_element_type=F32, **kw
    )


def shifted(block, axis, distance):
    size = lax.axis_size(axis)
    return lax.ppermute(block, axis, [(i, (i + distance) % size) for i in range(size)])


def join_kernel(values_ref, keys_ref, joined_ref, sems):
    hd = values_ref.shape[1]
    copies = [
        pltpu.make_async_copy(values_ref, joined_ref.at[:, pl.ds(0, hd)], sems.at[0]),
        pltpu.make_async_copy(keys_ref, joined_ref.at[:, pl.ds(hd, hd)], sems.at[1]),
    ]
    for copy in copies:
        copy.start()
    for copy in copies:
        copy.wait()


def halves_kernel(before_ref, after_ref, top_ref, bottom_ref, sems):
    half = top_ref.shape[0]
    copies = [
        pltpu.make_async_copy(before_ref.at[pl.ds(0, half)], top_ref, sems.at[0]),
        pltpu.make_async_copy(after_ref.at[pl.ds(half, half)], bottom_ref, sems.at[1]),
    ]
    for copy in copies:
        copy.start()
    for copy in copies:
        copy.wait()


def plan_kernel(
    index_ref, position_hbm, doc_hbm, plan_ref, home_doc_ref, home_pos_ref, position_ref, doc_ref, sems
):
    fetch = [
        pltpu.make_async_copy(doc_hbm, doc_ref, sems.at[0]),
        pltpu.make_async_copy(position_hbm, position_ref, sems.at[1]),
    ]
    for copy in fetch:
        copy.start()
    for copy in fetch:
        copy.wait()
    plan_attention(index_ref[0], index_ref[1], position_ref, doc_ref, plan_ref, home_doc_ref, home_pos_ref)


def plan_attention(x, z_y, position_ref, doc_ref, plan_ref, home_doc_ref, home_pos_ref):
    docs = doc_ref[...]
    begin = [jnp.sum(jnp.where(docs < doc, 1.0, 0.0).astype(F32), axis=0, keepdims=True) for doc in range(32)]
    begin = jnp.sum(jnp.concatenate(begin, axis=0), axis=1, keepdims=True)
    picks = lax.broadcasted_iota(jnp.int32, (16, 1024), 1) == STRIPE * lax.broadcasted_iota(jnp.int32, (16, 1024), 0)
    group = position_ref[pl.ds(pl.multiple_of(z_y // 2 * 8, 8), 8), :].astype(F32)
    group = jnp.where(z_y % 2 == 0, group[0:4], group[4:8])
    base = jnp.concatenate(
        [jnp.sum(jnp.where(picks, group[k : k + 1], 0.0), axis=1, keepdims=True) for k in range(4)], axis=0
    )
    t = lax.broadcasted_iota(jnp.int32, (64, 1), 0)
    away = (t // 16 + 4 - x) % 4
    shard = jnp.where(away == 0, 0, jnp.where(away == 1, 2, jnp.where(away == 2, 3, 1)))
    packed = base * 64.0 + (shard * 16 + t % 16).astype(F32)
    lane = lax.broadcasted_iota(jnp.int32, (1, 128), 1)
    doc_number = lax.broadcasted_iota(jnp.int32, (32, 32), 0)
    every_first = position_ref[:, 0:128].astype(F32)[:, 0:1]
    mine = lax.broadcasted_iota(jnp.int32, (32, 128), 0) == 4 * lax.broadcasted_iota(jnp.int32, (32, 128), 1) + x
    firsts = jnp.sum(jnp.where(mine, every_first, 0.0), axis=0, keepdims=True)
    low = jnp.zeros((1, 128), F32)
    home_doc = jnp.zeros((1, 32), jnp.int32)
    starts = []
    for b in range(8):
        first = jnp.sum(firsts[:, b : b + 1]).astype(jnp.int32)
        line = doc_ref[pl.ds(first // 128, 1), :]
        doc_row = jnp.where(first % 128 == 0, line[:, 0:32], line[:, 64:96])
        start = jnp.sum(jnp.where(doc_row == doc_number, begin, 0.0), axis=0, keepdims=True)
        starts.append(start)
        home_doc = home_doc + jnp.where(z_y == b, doc_row, 0)
        low = low + jnp.where(lane == b, start[:, 0:1], 0.0)
    diagonal = doc_number == lax.broadcasted_iota(jnp.int32, (32, 32), 1)
    home_doc = jnp.sum(jnp.where(diagonal, home_doc.astype(F32), 0.0), axis=1, keepdims=True)
    home_doc_ref[...] = jnp.broadcast_to(home_doc, (32, 128)).astype(jnp.int32)
    home_first = jnp.sum(jnp.where(lane == z_y, firsts, 0.0), axis=1, keepdims=True)
    home_pos_ref[...] = home_first + lax.broadcasted_iota(jnp.int32, (32, 128), 0).astype(F32)
    low = jnp.floor(low / STRIPE) * STRIPE
    need = jnp.where((base >= low) & (base <= firsts), 1.0, 0.0)
    below = lax.broadcasted_iota(jnp.int32, (64, 64), 1) <= lax.broadcasted_iota(jnp.int32, (64, 64), 0)
    rank = jnp.dot(
        jnp.where(below, 1.0, 0.0).astype(BF16), need.astype(BF16), preferred_element_type=F32
    )
    slot = (lane + 1).astype(F32)
    for b in range(8):
        chosen = (rank[:, b : b + 1] == slot) & (need[:, b : b + 1] > 0.0)
        row = jnp.sum(jnp.where(chosen, packed, 0.0), axis=0, keepdims=True)
        row = jnp.where(lane == 64, rank[63:64, b : b + 1], row)
        row = jnp.where(lane == 65, firsts[:, b : b + 1], row)
        row = jnp.concatenate([row[:, 0:96], starts[b]], axis=1)
        plan_ref[b : b + 1, :] = row.astype(jnp.int32)
    spot = lane.astype(F32)
    done, item = jnp.zeros((1, 1), F32), jnp.zeros((1, 128), F32)
    for b in range(8):
        after = done + jnp.floor((rank[63:64, b : b + 1] + (CHUNK - 1)) / CHUNK)
        item = item + jnp.where((spot >= done) & (spot < after), b * 16 + spot - done, 0.0)
        done = after
    item = jnp.where(spot >= done, 8.0 * 16, item)
    plan_ref[8:9, :] = item.astype(jnp.int32)
    plan_ref[9:10, :] = jnp.broadcast_to(done, (1, 128)).astype(jnp.int32)


PAIR = 2


def attend_kernel(heads, plan_rows_ref, left_ref, qd_hbm, *refs):
    kv_refs, out_hbm, plan_ref, qd_ref, kv_all, kv_now, acc_ref, top_ref, sum_ref, out_ref, sems, out_sems = (
        refs[:5],
        *refs[5:],
    )
    blocks, rows = qd_ref.shape[0:2]
    hd = 128
    width = heads * hd
    tall = rows * heads
    keys = CHUNK * STRIPE
    scale = 1.0 / math.sqrt(hd)

    copies = [
        pltpu.make_async_copy(plan_rows_ref, plan_ref, sems.at[5]),
        pltpu.make_async_copy(qd_hbm, qd_ref, sems.at[6]),
    ]
    row = 0
    for j, part in enumerate(kv_refs):
        copies.append(pltpu.make_async_copy(part, kv_all.at[pl.ds(row, part.shape[0])], sems.at[j]))
        row += part.shape[0]
    for copy in copies:
        copy.start()

    def clear(b, _):
        acc_ref[b] = jnp.zeros((tall, 3 * hd), F32)
        top_ref[b] = jnp.full((tall, 128), EMPTY, F32)
        sum_ref[b] = jnp.zeros((tall, 128), F32)
        return 0

    lax.fori_loop(0, blocks, clear, 0)
    for copy in copies:
        copy.wait()

    lane = lax.broadcasted_iota(jnp.int32, (1, keys), 1)
    diagonal = lax.broadcasted_iota(jnp.int32, (rows, rows), 0) == lax.broadcasted_iota(jnp.int32, (rows, rows), 1)
    row_i = lax.broadcasted_iota(jnp.int32, (rows, 1), 0)

    def wide(column):
        return jnp.broadcast_to(column, (tall, 128))

    def local_sums(i, item):
        held = item // 16
        c = item % 16
        b = jnp.minimum(held, blocks - 1)
        n = jnp.where(held < blocks, plan_ref[b, 64], 0)
        start = plan_rows_ref[pl.ds(b, 1), :][:, 96 : 96 + rows].astype(F32)
        start = jnp.sum(jnp.where(diagonal, start, 0.0), axis=1, keepdims=True).astype(jnp.int32)
        here = plan_ref[b, 65] + row_i
        key_pos = lane % STRIPE
        for u in range(CHUNK):
            slot = c * CHUNK + u
            valid = slot < n
            packed = plan_ref[b, jnp.minimum(slot, 63)]
            entry = jnp.where(valid, packed % 64, 0)
            base = jnp.where(valid, packed // 64, 1 << 24)
            kv_now[i, u * STRIPE : (u + 1) * STRIPE, :] = kv_all[pl.ds(pl.multiple_of(entry * STRIPE, STRIPE), STRIPE), :]
            key_pos = key_pos + jnp.where(lane // STRIPE == u, base, 0)
        bias = jnp.where((key_pos >= start) & (key_pos <= here), 0.0, MASKED).astype(F32)
        bias = jnp.concatenate([bias] * heads, axis=0)
        q, d = (
            jnp.concatenate(
                [qd_ref[b, :, side * width + h * hd : side * width + (h + 1) * hd] for h in range(heads)], axis=0
            )
            for side in range(2)
        )
        v, k = kv_now[i, :, 0:hd], kv_now[i, :, hd : 2 * hd]
        s = dot_t(q, k) * scale + bias
        dp = dot_t(d, v)
        top = jnp.maximum(wide(jnp.max(s, axis=1, keepdims=True)), EMPTY).astype(BF16).astype(F32)
        p = jnp.exp(s - jnp.concatenate([top, top], axis=1))
        total = wide(jnp.sum(p, axis=1, keepdims=True))
        pb = p.astype(BF16)
        w = (pb.astype(F32) * dp).astype(BF16)
        attn = jnp.dot(pb, kv_now[i], preferred_element_type=F32)
        grad = jnp.dot(w, k, preferred_element_type=F32)
        return held, top, total, (attn[:, 0:hd], attn[:, hd:], grad)

    def merge(held, top, total, sums):
        b = jnp.minimum(held, blocks)
        old = top_ref[b]
        new = jnp.maximum(old, top)
        keep, add = jnp.exp(old - new), jnp.exp(top - new)
        top_ref[b] = new
        sum_ref[b] = sum_ref[b] * keep + total * add
        for j, part in enumerate(sums):
            cols = slice(j * hd, (j + 1) * hd)
            acc_ref[b, :, cols] = acc_ref[b, :, cols] * keep + part * add

    def step(i, _):
        parts = [local_sums(j, plan_ref[8, i * PAIR + j]) for j in range(PAIR)]
        for part in parts:
            merge(*part)
        return 0

    lax.fori_loop(0, (plan_ref[9, 0] + PAIR - 1) // PAIR, step, 0)
    stat_lane = lax.broadcasted_iota(jnp.int32, (rows, 128), 1) - 64
    projected = []
    for h in range(heads):
        attn = acc_ref[0:blocks, h * rows : (h + 1) * rows, 0:hd].reshape(blocks * rows, hd).astype(BF16)
        projected.append(dot_t(attn, left_ref[:, h * hd : (h + 1) * hd].astype(BF16)))
    projected.append(jnp.zeros_like(projected[0]))
    for h in range(0, heads, 2):
        pair = jnp.concatenate(projected[h : h + 2], axis=1).astype(BF16)
        place = heads * 2 * hd + h // 2 * hd
        out_ref[:, :, place : place + hd] = pair.reshape(blocks, rows, hd)

    for b in range(blocks):
        stats = jnp.zeros((rows, 128), F32)
        for h in range(heads):
            part = slice(h * rows, (h + 1) * rows)
            out_ref[b, :, h * 2 * hd : (h + 1) * 2 * hd] = acc_ref[b, part, hd:].astype(BF16)
            d = qd_ref[b, :, width + h * hd : width + (h + 1) * hd].astype(F32)
            delta = jnp.sum(d * acc_ref[b, part, 0:hd], axis=1, keepdims=True)
            for place, value in enumerate((top_ref[b, part, :], sum_ref[b, part, :], delta)):
                stats = jnp.where(stat_lane == place * STAT + h, value, stats)
        high = stats.astype(BF16)
        low = pltpu.roll(stats - high.astype(F32), 32, 1).astype(BF16)
        last = heads * 2 * hd + heads // 2 * hd
        out_ref[b, :, last : last + 128] = jnp.where(
            stat_lane < 0, out_ref[b, :, last : last + 128], jnp.where(stat_lane < 32, high, low)
        )
        pltpu.make_async_copy(out_ref.at[b], out_hbm.at[b], out_sems.at[b]).start()
    for b in range(blocks):
        pltpu.make_async_copy(out_ref.at[b], out_hbm.at[b], out_sems.at[b]).wait()


def combine_kernel(heads, part_ref, cos_ref, sin_ref, right_ref, grad_ref, tail_ref):
    blocks = part_ref.shape[0]
    hd = 128
    low_half = lax.broadcasted_iota(jnp.int32, (part_ref.shape[1], hd), 1) < 64
    stat = heads * 2 * hd + heads // 2 * hd + 64
    stats = [part_ref[r, :, stat - 64 : stat + 64].astype(F32) for r in range(blocks)]
    stats = [s[:, 64:96] + s[:, 96:128] for s in stats]
    field = lambda s, place: s[:, place * STAT : (place + 1) * STAT]
    tops = [field(s, 0) for s in stats]
    top = functools.reduce(jnp.maximum, tops)
    weights = [jnp.exp(t - top) for t in tops]
    total = sum(w * field(s, 1) for w, s in zip(weights, stats))
    total = jnp.where(lax.broadcasted_iota(jnp.int32, total.shape, 1) < heads, total, 1.0)
    weights = [w / total for w in weights]
    delta = sum(w * field(s, 2) for w, s in zip(weights, stats))
    scale = 1.0 / math.sqrt(hd)
    cos, sin = cos_ref[...], sin_ref[...]
    for h in range(heads):
        whole = sum(
            weights[r][:, h : h + 1] * part_ref[r, :, h * 2 * hd : (h + 1) * 2 * hd].astype(F32)
            for r in range(blocks)
        )
        raw = (whole[:, hd:] - delta[:, h : h + 1] * whole[:, 0:hd]) * scale
        turned = jnp.concatenate([raw[:, hd // 2 :], raw[:, : hd // 2]], axis=1)
        grad_ref[:, h * hd : (h + 1) * hd] = (raw * cos + turned * sin).astype(BF16)
    tail_ref[:, 0:64] = dot_t(grad_ref[...], right_ref[...].astype(BF16))
    both = jnp.zeros((part_ref.shape[1], hd), F32)
    for r in range(blocks):
        for h in range(0, heads, 2):
            place = heads * 2 * hd + h // 2 * hd
            high = weights[r][:, h + 1 : h + 2] if h + 1 < heads else 0.0
            weight = jnp.where(low_half, weights[r][:, h : h + 1], high)
            both = both + weight * part_ref[r, :, place : place + hd].astype(F32)
    tail_ref[:, 64:128] = both[:, 0:64] + both[:, 64:128]


def docs_kernel(index_ref, head_ref, q_left_ref, o_right_ref, doc_ref, out_ref):
    h = index_ref[2]
    whole = head_ref[0] + head_ref[1] + head_ref[2] + head_ref[3]
    q_right, o_left_all = whole[:, 0:64], whole[:, 64:128]
    o_left = jnp.zeros((whole.shape[0], 16), F32)
    for k in range(4):
        o_left = o_left + jnp.where(h == k, o_left_all[:, 16 * k : 16 * k + 16], 0.0)
    doc = doc_ref[...]
    lane = lax.broadcasted_iota(jnp.int32, (whole.shape[0], 512), 1)
    mine = doc[:, 0:1] == lane // 16

    def split(value):
        high = value.astype(BF16)
        return high, (value - high.astype(F32)).astype(BF16)

    def outer(left, right):
        return lax.dot_general(left, right, (((0,), (0,)), ((), ())), preferred_element_type=F32)

    def terms(left, right):
        tiled = jnp.concatenate([left] * 8, axis=1)
        tiled = jnp.concatenate([tiled] * 4, axis=1)
        high, low = split(jnp.where(mine, tiled, 0.0))
        right_high, right_low = split(right)
        wide = outer(high, jnp.concatenate([right_high, right_low], axis=1))
        return wide[:, 0:64] + wide[:, 64:128] + outer(low, right_high)

    both = jnp.concatenate([terms(q_left_ref[...], q_right), terms(o_left, o_right_ref[...])], axis=1)
    out_ref[...] = both.reshape(out_ref.shape).astype(out_ref.dtype)


def total_kernel(part_ref, q_ref, o_ref):
    total = jnp.sum(part_ref[...].astype(F32), axis=0)
    for k in range(8):
        for side, ref in ((0, q_ref), (64, o_ref)):
            pair = [total[2 * k + j : 2 * k + j + 1, side : side + 64] for j in range(2)]
            ref[:, 128 * k : 128 * k + 128] = jnp.concatenate(pair, axis=1)


def call(kernel, out_shape, in_specs, out_specs, limit=LIMIT, **kw):
    return pl.pallas_call(
        kernel,
        out_shape=out_shape,
        in_specs=in_specs,
        out_specs=out_specs,
        compiler_params=pltpu.CompilerParams(vmem_limit_bytes=limit),
        **kw,
    )


def per_device(
    queries, keys, values, hidden_in, out_grad, w_out, q_left, q_right, o_left, o_right, positions, doc_ids
):
    shape = jax.ShapeDtypeStruct
    rows, width = queries.shape
    hd = keys.shape[1]
    heads = width // hd
    blocks = 8
    z, y, x, head = (lax.axis_index(a) for a in ("z", "y", "x", "head"))
    seq = (z * 2 + y) * 4 + x

    anywhere = pl.BlockSpec(memory_space=pl.ANY)
    kv = call(
        join_kernel,
        shape((keys.shape[0], 2 * hd), BF16),
        [anywhere] * 2,
        anywhere,
        scratch_shapes=[pltpu.SemaphoreType.DMA((2,))],
        cost_estimate=pl.CostEstimate(flops=40 << 30, bytes_accessed=64 << 20, transcendentals=0),
    )(values, keys)
    kv_before = shifted(kv, "x", 1)
    kv_after = shifted(kv, "x", -1)
    half = shape((kv.shape[0] // 2, kv.shape[1]), BF16)
    anywhere = pl.BlockSpec(memory_space=pl.ANY)
    top, bottom = call(
        halves_kernel,
        (half, half),
        [anywhere] * 2,
        (anywhere, anywhere),
        scratch_shapes=[pltpu.SemaphoreType.DMA((2,))],
        cost_estimate=pl.CostEstimate(flops=40 << 30, bytes_accessed=64 << 20, transcendentals=0),
    )(kv_before, kv_after)
    far_top = shifted(top, "x", 1)
    far_bottom = shifted(bottom, "x", -1)

    hbm = pl.BlockSpec(memory_space=pltpu.HBM)
    index = jnp.stack([x, z * 2 + y, head]).astype(jnp.int32)
    attn_grad = dot_t(out_grad, w_out).astype(BF16)
    o_side = dot_t(out_grad, o_right)
    attn_grad, o_side = lax.optimization_barrier((attn_grad, o_side))
    mine = jnp.concatenate([queries, attn_grad], axis=1)
    qd = lax.all_to_all(jnp.broadcast_to(mine[None], (blocks,) + mine.shape), FAR, 0, 0)

    plan, home_doc, home_pos = call(
        plan_kernel,
        (shape((16, 128), jnp.int32), shape((rows, 128), jnp.int32), shape((rows, 128), F32)),
        [SMEM, hbm, hbm],
        (VMEM, VMEM, VMEM),
        scratch_shapes=[
            pltpu.VMEM(positions.shape, jnp.int32),
            pltpu.VMEM((256, 128), jnp.int32),
            pltpu.SemaphoreType.DMA((2,)),
        ],
    )(index, positions, doc_ids.reshape(256, 128))

    q_left_rows = lax.dynamic_slice_in_dim(q_left, head * 16, 16)
    q_side = dot_t(hidden_in, q_left_rows)

    out_lanes = heads * 2 * hd + (heads + 1) // 2 * hd
    tall = heads * rows
    parts = call(
        functools.partial(attend_kernel, heads),
        shape((blocks, rows, out_lanes), BF16),
        [VMEM] * 2 + [anywhere] * 6,
        anywhere,
        scratch_shapes=[
            pltpu.SMEM((16, 128), jnp.int32),
            pltpu.VMEM((blocks, rows, 2 * width), BF16),
            pltpu.VMEM((4096, 2 * hd), BF16),
            pltpu.VMEM((PAIR, CHUNK * STRIPE, 2 * hd), BF16),
            pltpu.VMEM((blocks + 1, tall, 3 * hd), F32),
            pltpu.VMEM((blocks + 1, tall, 128), F32),
            pltpu.VMEM((blocks + 1, tall, 128), F32),
            pltpu.VMEM((blocks, rows, out_lanes), BF16),
            pltpu.SemaphoreType.DMA((7,)),
            pltpu.SemaphoreType.DMA((blocks,)),
        ],
        limit=ATTEND_LIMIT,
    )(plan, o_left.astype(F32), qd, kv, kv_before, kv_after, far_top, far_bottom)
    parts = lax.all_to_all(parts, FAR, 0, 0)

    inverse_freq = ROPE_BASE ** (-(jnp.arange(hd // 2, dtype=F32) * 2.0) / hd)
    angles = home_pos * jnp.concatenate([inverse_freq, inverse_freq])[None, :]
    sign = jnp.where(jnp.arange(hd) < hd // 2, 1.0, -1.0).astype(F32)[None, :]
    query_grad, tail = call(
        functools.partial(combine_kernel, heads),
        (shape((rows, width), BF16), shape((rows, 128), F32)),
        [VMEM] * 4,
        (VMEM, VMEM),
    )(
        parts,
        jnp.cos(angles),
        jnp.sin(angles) * sign,
        q_right.astype(F32),
    )

    by_doc = call(
        docs_kernel,
        shape((32, 16, 128), BF16),
        [SMEM] + [VMEM] * 4,
        VMEM,
    )(index, lax.all_gather(tail, "head"), q_side, o_side, home_doc)
    by_doc = lax.all_to_all(by_doc, SEQ_AXES, 0, 0)
    q_docs, o_docs = call(
        total_kernel, (shape((1, 1024), F32), shape((1, 1024), F32)), [VMEM], (VMEM, VMEM)
    )(by_doc)
    return (query_grad, q_docs, o_docs)


def solution(mesh):
    grid = Mesh(mesh.devices.reshape(4, 2, 4, 4), ("z", "y", "x", "head"))
    both, seq, head = P(SEQ_AXES, "head"), P(SEQ_AXES, None), P("head", None)
    placed = (both, both, both, seq, seq, head, P(), P(None, "head"), P(None, "head"), P(), P(), P())
    return jax.shard_map(
        per_device, mesh=grid, in_specs=placed, out_specs=(both, both, both), check_vma=False
    )
```

```python
import functools
import math

import jax
import jax.numpy as jnp
from jax import lax
from jax.experimental import pallas as pl
from jax.experimental.pallas import tpu as pltpu
from jax.sharding import Mesh
from jax.sharding import PartitionSpec as P

ROPE_BASE = 10000000.0
MASKED = -1e30
EMPTY = -1e20
STRIPE = 64
CHUNK = 4
STAT = 8
F32 = jnp.float32
BF16 = jnp.bfloat16

SEQ_AXES = ("z", "y", "x")
FAR = ("z", "y")
VMEM = pl.BlockSpec(memory_space=pltpu.VMEM)
SMEM = pl.BlockSpec(memory_space=pltpu.SMEM)
LIMIT = 12 * 1024 * 1024
ATTEND_LIMIT = 24 * 1024 * 1024


def dot_t(left, right, **kw):
    return lax.dot_general(
        left, right, (((1,), (1,)), ((), ())), preferred_element_type=F32, **kw
    )


def shifted(block, axis, distance):
    size = lax.axis_size(axis)
    return lax.ppermute(block, axis, [(i, (i + distance) % size) for i in range(size)])


def join_kernel(values_ref, keys_ref, joined_ref, sems):
    hd = values_ref.shape[1]
    copies = [
        pltpu.make_async_copy(values_ref, joined_ref.at[:, pl.ds(0, hd)], sems.at[0]),
        pltpu.make_async_copy(keys_ref, joined_ref.at[:, pl.ds(hd, hd)], sems.at[1]),
    ]
    for copy in copies:
        copy.start()
    for copy in copies:
        copy.wait()


def halves_kernel(before_ref, after_ref, top_ref, bottom_ref, sems):
    half = top_ref.shape[0]
    copies = [
        pltpu.make_async_copy(before_ref.at[pl.ds(0, half)], top_ref, sems.at[0]),
        pltpu.make_async_copy(after_ref.at[pl.ds(half, half)], bottom_ref, sems.at[1]),
    ]
    for copy in copies:
        copy.start()
    for copy in copies:
        copy.wait()


def plan_kernel(
    index_ref, position_hbm, doc_hbm, plan_ref, home_doc_ref, home_pos_ref, position_ref, doc_ref, sems
):
    fetch = [
        pltpu.make_async_copy(doc_hbm, doc_ref, sems.at[0]),
        pltpu.make_async_copy(position_hbm, position_ref, sems.at[1]),
    ]
    for copy in fetch:
        copy.start()
    for copy in fetch:
        copy.wait()
    plan_attention(index_ref[0], index_ref[1], position_ref, doc_ref, plan_ref, home_doc_ref, home_pos_ref)


def plan_attention(x, z_y, position_ref, doc_ref, plan_ref, home_doc_ref, home_pos_ref):
    docs = doc_ref[...]
    begin = [jnp.sum(jnp.where(docs < doc, 1.0, 0.0).astype(F32), axis=0, keepdims=True) for doc in range(32)]
    begin = jnp.sum(jnp.concatenate(begin, axis=0), axis=1, keepdims=True)
    picks = lax.broadcasted_iota(jnp.int32, (16, 1024), 1) == STRIPE * lax.broadcasted_iota(jnp.int32, (16, 1024), 0)
    group = position_ref[pl.ds(pl.multiple_of(z_y // 2 * 8, 8), 8), :].astype(F32)
    group = jnp.where(z_y % 2 == 0, group[0:4], group[4:8])
    base = jnp.concatenate(
        [jnp.sum(jnp.where(picks, group[k : k + 1], 0.0), axis=1, keepdims=True) for k in range(4)], axis=0
    )
    t = lax.broadcasted_iota(jnp.int32, (64, 1), 0)
    away = (t // 16 + 4 - x) % 4
    shard = jnp.where(away == 0, 0, jnp.where(away == 1, 2, jnp.where(away == 2, 3, 1)))
    packed = base * 64.0 + (shard * 16 + t % 16).astype(F32)
    lane = lax.broadcasted_iota(jnp.int32, (1, 128), 1)
    doc_number = lax.broadcasted_iota(jnp.int32, (32, 32), 0)
    every_first = position_ref[:, 0:128].astype(F32)[:, 0:1]
    mine = lax.broadcasted_iota(jnp.int32, (32, 128), 0) == 4 * lax.broadcasted_iota(jnp.int32, (32, 128), 1) + x
    firsts = jnp.sum(jnp.where(mine, every_first, 0.0), axis=0, keepdims=True)
    low = jnp.zeros((1, 128), F32)
    home_doc = jnp.zeros((1, 32), jnp.int32)
    starts = []
    for b in range(8):
        first = jnp.sum(firsts[:, b : b + 1]).astype(jnp.int32)
        line = doc_ref[pl.ds(first // 128, 1), :]
        doc_row = jnp.where(first % 128 == 0, line[:, 0:32], line[:, 64:96])
        start = jnp.sum(jnp.where(doc_row == doc_number, begin, 0.0), axis=0, keepdims=True)
        starts.append(start)
        home_doc = home_doc + jnp.where(z_y == b, doc_row, 0)
        low = low + jnp.where(lane == b, start[:, 0:1], 0.0)
    diagonal = doc_number == lax.broadcasted_iota(jnp.int32, (32, 32), 1)
    home_doc = jnp.sum(jnp.where(diagonal, home_doc.astype(F32), 0.0), axis=1, keepdims=True)
    home_doc_ref[...] = jnp.broadcast_to(home_doc, (32, 128)).astype(jnp.int32)
    home_first = jnp.sum(jnp.where(lane == z_y, firsts, 0.0), axis=1, keepdims=True)
    home_pos_ref[...] = home_first + lax.broadcasted_iota(jnp.int32, (32, 128), 0).astype(F32)
    low = jnp.floor(low / STRIPE) * STRIPE
    need = jnp.where((base >= low) & (base <= firsts), 1.0, 0.0)
    below = lax.broadcasted_iota(jnp.int32, (64, 64), 1) <= lax.broadcasted_iota(jnp.int32, (64, 64), 0)
    rank = jnp.dot(
        jnp.where(below, 1.0, 0.0).astype(BF16), need.astype(BF16), preferred_element_type=F32
    )
    slot = (lane + 1).astype(F32)
    for b in range(8):
        chosen = (rank[:, b : b + 1] == slot) & (need[:, b : b + 1] > 0.0)
        row = jnp.sum(jnp.where(chosen, packed, 0.0), axis=0, keepdims=True)
        row = jnp.where(lane == 64, rank[63:64, b : b + 1], row)
        row = jnp.where(lane == 65, firsts[:, b : b + 1], row)
        row = jnp.concatenate([row[:, 0:96], starts[b]], axis=1)
        plan_ref[b : b + 1, :] = row.astype(jnp.int32)
    spot = lane.astype(F32)
    done, item = jnp.zeros((1, 1), F32), jnp.zeros((1, 128), F32)
    for b in range(8):
        after = done + jnp.floor((rank[63:64, b : b + 1] + (CHUNK - 1)) / CHUNK)
        item = item + jnp.where((spot >= done) & (spot < after), b * 16 + spot - done, 0.0)
        done = after
    item = jnp.where(spot >= done, 8.0 * 16, item)
    plan_ref[8:9, :] = item.astype(jnp.int32)
    plan_ref[9:10, :] = jnp.broadcast_to(done, (1, 128)).astype(jnp.int32)


PAIR = 4


def attend_kernel(heads, plan_rows_ref, left_ref, qd_hbm, *refs):
    kv_refs, out_hbm, plan_ref, qd_ref, kv_all, kv_now, acc_ref, top_ref, sum_ref, out_ref, sems, out_sems = (
        refs[:5],
        *refs[5:],
    )
    blocks, rows = qd_ref.shape[0:2]
    hd = 128
    width = heads * hd
    tall = rows * heads
    keys = CHUNK * STRIPE
    scale = 1.0 / math.sqrt(hd)

    copies = [
        pltpu.make_async_copy(plan_rows_ref, plan_ref, sems.at[5]),
        pltpu.make_async_copy(qd_hbm, qd_ref, sems.at[6]),
    ]
    row = 0
    for j, part in enumerate(kv_refs):
        copies.append(pltpu.make_async_copy(part, kv_all.at[pl.ds(row, part.shape[0])], sems.at[j]))
        row += part.shape[0]
    for copy in copies:
        copy.start()

    def clear(b, _):
        acc_ref[b] = jnp.zeros((tall, 3 * hd), F32)
        top_ref[b] = jnp.full((tall, 128), EMPTY, F32)
        sum_ref[b] = jnp.zeros((tall, 128), F32)
        return 0

    lax.fori_loop(0, blocks, clear, 0)
    for copy in copies:
        copy.wait()

    lane = lax.broadcasted_iota(jnp.int32, (1, keys), 1)
    diagonal = lax.broadcasted_iota(jnp.int32, (rows, rows), 0) == lax.broadcasted_iota(jnp.int32, (rows, rows), 1)
    row_i = lax.broadcasted_iota(jnp.int32, (rows, 1), 0)

    def wide(column):
        return jnp.broadcast_to(column, (tall, 128))

    def scores(i, item):
        held = item // 16
        c = item % 16
        b = jnp.minimum(held, blocks - 1)
        n = jnp.where(held < blocks, plan_ref[b, 64], 0)
        start = plan_rows_ref[pl.ds(b, 1), :][:, 96 : 96 + rows].astype(F32)
        start = jnp.sum(jnp.where(diagonal, start, 0.0), axis=1, keepdims=True).astype(jnp.int32)
        here = plan_ref[b, 65] + row_i
        key_pos = lane % STRIPE
        for u in range(CHUNK):
            slot = c * CHUNK + u
            valid = slot < n
            packed = plan_ref[b, jnp.minimum(slot, 63)]
            entry = jnp.where(valid, packed % 64, 0)
            base = jnp.where(valid, packed // 64, 1 << 24)
            kv_now[i, u * STRIPE : (u + 1) * STRIPE, :] = kv_all[pl.ds(pl.multiple_of(entry * STRIPE, STRIPE), STRIPE), :]
            key_pos = key_pos + jnp.where(lane // STRIPE == u, base, 0)
        bias = jnp.where((key_pos >= start) & (key_pos <= here), 0.0, MASKED).astype(F32)
        bias = jnp.concatenate([bias] * heads, axis=0)
        q, d = (
            jnp.concatenate(
                [qd_ref[b, :, side * width + h * hd : side * width + (h + 1) * hd] for h in range(heads)], axis=0
            )
            for side in range(2)
        )
        s = dot_t(q, kv_now[i, :, hd : 2 * hd]) * scale + bias
        return held, s, dot_t(d, kv_now[i, :, 0:hd])

    def softmax(held, s, dp):
        top = jnp.maximum(wide(jnp.max(s, axis=1, keepdims=True)), EMPTY).astype(BF16).astype(F32)
        p = jnp.exp(s - jnp.concatenate([top, top], axis=1))
        total = wide(jnp.sum(p, axis=1, keepdims=True))
        pb = p.astype(BF16)
        return held, top, total, pb, (pb.astype(F32) * dp).astype(BF16)

    def products(i, held, top, total, pb, w):
        attn = jnp.dot(pb, kv_now[i], preferred_element_type=F32)
        grad = jnp.dot(w, kv_now[i, :, hd : 2 * hd], preferred_element_type=F32)
        return held, top, total, (attn[:, 0:hd], attn[:, hd:], grad)

    def merge(held, top, total, sums):
        b = jnp.minimum(held, blocks)
        old = top_ref[b]
        new = jnp.maximum(old, top)
        keep, add = jnp.exp(old - new), jnp.exp(top - new)
        top_ref[b] = new
        sum_ref[b] = sum_ref[b] * keep + total * add
        for j, part in enumerate(sums):
            cols = slice(j * hd, (j + 1) * hd)
            acc_ref[b, :, cols] = acc_ref[b, :, cols] * keep + part * add

    def step(i, _):
        parts = [scores(j, plan_ref[8, i * PAIR + j]) for j in range(PAIR)]
        parts = [softmax(*part) for part in parts]
        parts = [products(j, *part) for j, part in enumerate(parts)]
        for part in parts:
            merge(*part)
        return 0

    lax.fori_loop(0, (plan_ref[9, 0] + PAIR - 1) // PAIR, step, 0)
    stat_lane = lax.broadcasted_iota(jnp.int32, (rows, 128), 1) - 64
    projected = []
    for h in range(heads):
        attn = acc_ref[0:blocks, h * rows : (h + 1) * rows, 0:hd].reshape(blocks * rows, hd).astype(BF16)
        projected.append(dot_t(attn, left_ref[:, h * hd : (h + 1) * hd].astype(BF16)))
    projected.append(jnp.zeros_like(projected[0]))
    for h in range(0, heads, 2):
        pair = jnp.concatenate(projected[h : h + 2], axis=1).astype(BF16)
        place = heads * 2 * hd + h // 2 * hd
        out_ref[:, :, place : place + hd] = pair.reshape(blocks, rows, hd)

    ones = jnp.ones((hd, 128), BF16)
    deltas = []
    for b in range(blocks):
        d = jnp.concatenate([qd_ref[b, :, width + h * hd : width + (h + 1) * hd] for h in range(heads)], axis=0)
        terms = d.astype(F32) * acc_ref[b, :, 0:hd]
        high = terms.astype(BF16)
        low = (terms - high.astype(F32)).astype(BF16)
        both = jnp.dot(jnp.concatenate([high, low], axis=0), ones, preferred_element_type=F32)
        deltas.append(both[0:tall] + both[tall:])
    for b in range(blocks):
        stats = jnp.zeros((rows, 128), F32)
        for h in range(heads):
            part = slice(h * rows, (h + 1) * rows)
            out_ref[b, :, h * 2 * hd : (h + 1) * 2 * hd] = acc_ref[b, part, hd:].astype(BF16)
            for place, value in enumerate((top_ref[b, part, :], sum_ref[b, part, :], deltas[b][part])):
                stats = jnp.where(stat_lane == place * STAT + h, value, stats)
        high = stats.astype(BF16)
        low = pltpu.roll(stats - high.astype(F32), 32, 1).astype(BF16)
        last = heads * 2 * hd + heads // 2 * hd
        out_ref[b, :, last : last + 128] = jnp.where(
            stat_lane < 0, out_ref[b, :, last : last + 128], jnp.where(stat_lane < 32, high, low)
        )
        pltpu.make_async_copy(out_ref.at[b], out_hbm.at[b], out_sems.at[b]).start()
    for b in range(blocks):
        pltpu.make_async_copy(out_ref.at[b], out_hbm.at[b], out_sems.at[b]).wait()


def combine_kernel(heads, part_ref, cos_ref, sin_ref, right_ref, grad_ref, tail_ref):
    blocks = part_ref.shape[0]
    hd = 128
    low_half = lax.broadcasted_iota(jnp.int32, (part_ref.shape[1], hd), 1) < 64
    stat = heads * 2 * hd + heads // 2 * hd + 64
    stats = [part_ref[r, :, stat - 64 : stat + 64].astype(F32) for r in range(blocks)]
    stats = [s[:, 64:96] + s[:, 96:128] for s in stats]
    field = lambda s, place: s[:, place * STAT : (place + 1) * STAT]
    tops = [field(s, 0) for s in stats]
    top = functools.reduce(jnp.maximum, tops)
    weights = [jnp.exp(t - top) for t in tops]
    total = sum(w * field(s, 1) for w, s in zip(weights, stats))
    total = jnp.where(lax.broadcasted_iota(jnp.int32, total.shape, 1) < heads, total, 1.0)
    weights = [w / total for w in weights]
    delta = sum(w * field(s, 2) for w, s in zip(weights, stats))
    scale = 1.0 / math.sqrt(hd)
    cos, sin = cos_ref[...], sin_ref[...]
    wide = [[jnp.broadcast_to(w[:, h : h + 1], (w.shape[0], hd)) for h in range(heads)] for w in weights]
    for h in range(heads):
        key_sum, grad_sum = (
            sum(
                wide[r][h] * part_ref[r, :, (2 * h + side) * hd : (2 * h + side + 1) * hd].astype(F32)
                for r in range(blocks)
            )
            for side in range(2)
        )
        raw = (grad_sum - delta[:, h : h + 1] * key_sum) * scale
        turned = jnp.concatenate([raw[:, hd // 2 :], raw[:, : hd // 2]], axis=1)
        grad_ref[:, h * hd : (h + 1) * hd] = (raw * cos + turned * sin).astype(BF16)
    tail_ref[:, 0:64] = dot_t(grad_ref[...], right_ref[...].astype(BF16))
    both = jnp.zeros((part_ref.shape[1], hd), F32)
    for r in range(blocks):
        for h in range(0, heads, 2):
            place = heads * 2 * hd + h // 2 * hd
            weight = jnp.where(low_half, wide[r][h], wide[r][h + 1] if h + 1 < heads else 0.0)
            both = both + weight * part_ref[r, :, place : place + hd].astype(F32)
    tail_ref[:, 64:128] = both[:, 0:64] + both[:, 64:128]


def docs_kernel(index_ref, head_ref, q_left_ref, o_right_ref, doc_ref, out_ref):
    h = index_ref[2]
    whole = head_ref[0] + head_ref[1] + head_ref[2] + head_ref[3]
    q_right, o_left_all = whole[:, 0:64], whole[:, 64:128]
    o_left = jnp.zeros((whole.shape[0], 16), F32)
    for k in range(4):
        o_left = o_left + jnp.where(h == k, o_left_all[:, 16 * k : 16 * k + 16], 0.0)
    doc = doc_ref[...]
    lane = lax.broadcasted_iota(jnp.int32, (whole.shape[0], 512), 1)
    mine = doc[:, 0:1] == lane // 16

    def split(value):
        high = value.astype(BF16)
        return high, (value - high.astype(F32)).astype(BF16)

    def outer(left, right):
        return lax.dot_general(left, right, (((0,), (0,)), ((), ())), preferred_element_type=F32)

    def terms(left, right):
        tiled = jnp.concatenate([left] * 8, axis=1)
        tiled = jnp.concatenate([tiled] * 4, axis=1)
        high, low = split(jnp.where(mine, tiled, 0.0))
        right_high, right_low = split(right)
        wide = outer(high, jnp.concatenate([right_high, right_low], axis=1))
        return wide[:, 0:64] + wide[:, 64:128] + outer(low, right_high)

    both = jnp.concatenate([terms(q_left_ref[...], q_right), terms(o_left, o_right_ref[...])], axis=1)
    out_ref[...] = both.reshape(out_ref.shape).astype(out_ref.dtype)


def total_kernel(part_ref, q_ref, o_ref):
    total = jnp.sum(part_ref[...].astype(F32), axis=0)
    for k in range(8):
        for side, ref in ((0, q_ref), (64, o_ref)):
            pair = [total[2 * k + j : 2 * k + j + 1, side : side + 64] for j in range(2)]
            ref[:, 128 * k : 128 * k + 128] = jnp.concatenate(pair, axis=1)


def call(kernel, out_shape, in_specs, out_specs, limit=LIMIT, **kw):
    return pl.pallas_call(
        kernel,
        out_shape=out_shape,
        in_specs=in_specs,
        out_specs=out_specs,
        compiler_params=pltpu.CompilerParams(vmem_limit_bytes=limit),
        **kw,
    )


def per_device(
    queries, keys, values, hidden_in, out_grad, w_out, q_left, q_right, o_left, o_right, positions, doc_ids
):
    shape = jax.ShapeDtypeStruct
    rows, width = queries.shape
    hd = keys.shape[1]
    heads = width // hd
    blocks = 8
    z, y, x, head = (lax.axis_index(a) for a in ("z", "y", "x", "head"))
    seq = (z * 2 + y) * 4 + x

    anywhere = pl.BlockSpec(memory_space=pl.ANY)
    kv = call(
        join_kernel,
        shape((keys.shape[0], 2 * hd), BF16),
        [anywhere] * 2,
        anywhere,
        scratch_shapes=[pltpu.SemaphoreType.DMA((2,))],
        cost_estimate=pl.CostEstimate(flops=40 << 30, bytes_accessed=64 << 20, transcendentals=0),
    )(values, keys)
    kv_before = shifted(kv, "x", 1)
    kv_after = shifted(kv, "x", -1)
    half = shape((kv.shape[0] // 2, kv.shape[1]), BF16)
    anywhere = pl.BlockSpec(memory_space=pl.ANY)
    top, bottom = call(
        halves_kernel,
        (half, half),
        [anywhere] * 2,
        (anywhere, anywhere),
        scratch_shapes=[pltpu.SemaphoreType.DMA((2,))],
        cost_estimate=pl.CostEstimate(flops=40 << 30, bytes_accessed=64 << 20, transcendentals=0),
    )(kv_before, kv_after)
    far_top = shifted(top, "x", 1)
    far_bottom = shifted(bottom, "x", -1)

    hbm = pl.BlockSpec(memory_space=pltpu.HBM)
    index = jnp.stack([x, z * 2 + y, head]).astype(jnp.int32)
    attn_grad = dot_t(out_grad, w_out).astype(BF16)
    o_side = dot_t(out_grad, o_right)
    attn_grad, o_side = lax.optimization_barrier((attn_grad, o_side))
    mine = jnp.concatenate([queries, attn_grad], axis=1)
    qd = lax.all_to_all(jnp.broadcast_to(mine[None], (blocks,) + mine.shape), FAR, 0, 0)

    plan, home_doc, home_pos = call(
        plan_kernel,
        (shape((16, 128), jnp.int32), shape((rows, 128), jnp.int32), shape((rows, 128), F32)),
        [SMEM, hbm, hbm],
        (VMEM, VMEM, VMEM),
        scratch_shapes=[
            pltpu.VMEM(positions.shape, jnp.int32),
            pltpu.VMEM((256, 128), jnp.int32),
            pltpu.SemaphoreType.DMA((2,)),
        ],
    )(index, positions, doc_ids.reshape(256, 128))

    q_left_rows = lax.dynamic_slice_in_dim(q_left, head * 16, 16)
    q_side = dot_t(hidden_in, q_left_rows)

    out_lanes = heads * 2 * hd + (heads + 1) // 2 * hd
    tall = heads * rows
    parts = call(
        functools.partial(attend_kernel, heads),
        shape((blocks, rows, out_lanes), BF16),
        [VMEM] * 2 + [anywhere] * 6,
        anywhere,
        scratch_shapes=[
            pltpu.SMEM((16, 128), jnp.int32),
            pltpu.VMEM((blocks, rows, 2 * width), BF16),
            pltpu.VMEM((4096, 2 * hd), BF16),
            pltpu.VMEM((PAIR, CHUNK * STRIPE, 2 * hd), BF16),
            pltpu.VMEM((blocks + 1, tall, 3 * hd), F32),
            pltpu.VMEM((blocks + 1, tall, 128), F32),
            pltpu.VMEM((blocks + 1, tall, 128), F32),
            pltpu.VMEM((blocks, rows, out_lanes), BF16),
            pltpu.SemaphoreType.DMA((7,)),
            pltpu.SemaphoreType.DMA((blocks,)),
        ],
        limit=ATTEND_LIMIT,
    )(plan, o_left.astype(F32), qd, kv, kv_before, kv_after, far_top, far_bottom)
    parts = lax.all_to_all(parts, FAR, 0, 0)

    inverse_freq = ROPE_BASE ** (-(jnp.arange(hd // 2, dtype=F32) * 2.0) / hd)
    angles = home_pos * jnp.concatenate([inverse_freq, inverse_freq])[None, :]
    sign = jnp.where(jnp.arange(hd) < hd // 2, 1.0, -1.0).astype(F32)[None, :]
    query_grad, tail = call(
        functools.partial(combine_kernel, heads),
        (shape((rows, width), BF16), shape((rows, 128), F32)),
        [VMEM] * 4,
        (VMEM, VMEM),
    )(
        parts,
        jnp.cos(angles),
        jnp.sin(angles) * sign,
        q_right.astype(F32),
    )

    by_doc = call(
        docs_kernel,
        shape((32, 16, 128), BF16),
        [SMEM] + [VMEM] * 4,
        VMEM,
    )(index, lax.all_gather(tail, "head"), q_side, o_side, home_doc)
    by_doc = lax.all_to_all(by_doc, SEQ_AXES, 0, 0)
    q_docs, o_docs = call(
        total_kernel, (shape((1, 1024), F32), shape((1, 1024), F32)), [VMEM], (VMEM, VMEM)
    )(by_doc)
    return (query_grad, q_docs, o_docs)


def solution(mesh):
    grid = Mesh(mesh.devices.reshape(4, 2, 4, 4), ("z", "y", "x", "head"))
    both, seq, head = P(SEQ_AXES, "head"), P(SEQ_AXES, None), P("head", None)
    placed = (both, both, both, seq, seq, head, P(), P(None, "head"), P(None, "head"), P(), P(), P())
    return jax.shard_map(
        per_device, mesh=grid, in_specs=placed, out_specs=(both, both, both), check_vma=False
    )
```

```python
import functools
import math

import jax
import jax.numpy as jnp
from jax import lax
from jax.experimental import pallas as pl
from jax.experimental.pallas import tpu as pltpu
from jax.sharding import Mesh
from jax.sharding import PartitionSpec as P

ROPE_BASE = 10000000.0
MASKED = -1e30
EMPTY = -1e20
STRIPE = 64
CHUNK = 4
STAT = 8
F32 = jnp.float32
BF16 = jnp.bfloat16

SEQ_AXES = ("z", "y", "x")
FAR = ("z", "y")
VMEM = pl.BlockSpec(memory_space=pltpu.VMEM)
SMEM = pl.BlockSpec(memory_space=pltpu.SMEM)
LIMIT = 12 * 1024 * 1024
ATTEND_LIMIT = 24 * 1024 * 1024


def dot_t(left, right, **kw):
    return lax.dot_general(
        left, right, (((1,), (1,)), ((), ())), preferred_element_type=F32, **kw
    )


def shifted(block, axis, distance):
    size = lax.axis_size(axis)
    return lax.ppermute(block, axis, [(i, (i + distance) % size) for i in range(size)])


def place_kernel(index_ref, same_ref):
    for i in range(3):
        same_ref[i] = index_ref[i]


def join_kernel(index_ref, values_ref, keys_ref, joined_ref, sems):
    hd = values_ref.shape[1]
    copies = [
        pltpu.make_async_copy(values_ref, joined_ref.at[:, pl.ds(0, hd)], sems.at[0]),
        pltpu.make_async_copy(keys_ref, joined_ref.at[:, pl.ds(hd, hd)], sems.at[1]),
    ]
    for copy in copies:
        copy.start()
    for copy in copies:
        copy.wait()


def halves_kernel(before_ref, after_ref, top_ref, bottom_ref, sems):
    half = top_ref.shape[0]
    copies = [
        pltpu.make_async_copy(before_ref.at[pl.ds(0, half)], top_ref, sems.at[0]),
        pltpu.make_async_copy(after_ref.at[pl.ds(half, half)], bottom_ref, sems.at[1]),
    ]
    for copy in copies:
        copy.start()
    for copy in copies:
        copy.wait()


def plan_kernel(
    index_ref, position_hbm, doc_hbm, plan_ref, home_doc_ref, home_pos_ref, position_ref, doc_ref, sems
):
    fetch = [
        pltpu.make_async_copy(doc_hbm, doc_ref, sems.at[0]),
        pltpu.make_async_copy(position_hbm, position_ref, sems.at[1]),
    ]
    for copy in fetch:
        copy.start()
    for copy in fetch:
        copy.wait()
    plan_attention(index_ref[0], index_ref[1], position_ref, doc_ref, plan_ref, home_doc_ref, home_pos_ref)


def plan_attention(x, z_y, position_ref, doc_ref, plan_ref, home_doc_ref, home_pos_ref):
    docs = doc_ref[...]
    begin = [jnp.sum(jnp.where(docs < doc, 1.0, 0.0).astype(F32), axis=0, keepdims=True) for doc in range(32)]
    begin = jnp.sum(jnp.concatenate(begin, axis=0), axis=1, keepdims=True)
    picks = lax.broadcasted_iota(jnp.int32, (16, 1024), 1) == STRIPE * lax.broadcasted_iota(jnp.int32, (16, 1024), 0)
    group = position_ref[pl.ds(pl.multiple_of(z_y // 2 * 8, 8), 8), :].astype(F32)
    group = jnp.where(z_y % 2 == 0, group[0:4], group[4:8])
    base = jnp.concatenate(
        [jnp.sum(jnp.where(picks, group[k : k + 1], 0.0), axis=1, keepdims=True) for k in range(4)], axis=0
    )
    t = lax.broadcasted_iota(jnp.int32, (64, 1), 0)
    away = (t // 16 + 4 - x) % 4
    shard = jnp.where(away == 0, 0, jnp.where(away == 1, 2, jnp.where(away == 2, 3, 1)))
    packed = base * 64.0 + (shard * 16 + t % 16).astype(F32)
    lane = lax.broadcasted_iota(jnp.int32, (1, 128), 1)
    doc_number = lax.broadcasted_iota(jnp.int32, (32, 32), 0)
    every_first = position_ref[:, 0:128].astype(F32)[:, 0:1]
    mine = lax.broadcasted_iota(jnp.int32, (32, 128), 0) == 4 * lax.broadcasted_iota(jnp.int32, (32, 128), 1) + x
    firsts = jnp.sum(jnp.where(mine, every_first, 0.0), axis=0, keepdims=True)
    low = jnp.zeros((1, 128), F32)
    home_doc = jnp.zeros((1, 32), jnp.int32)
    starts = []
    for b in range(8):
        first = jnp.sum(firsts[:, b : b + 1]).astype(jnp.int32)
        line = doc_ref[pl.ds(first // 128, 1), :]
        doc_row = jnp.where(first % 128 == 0, line[:, 0:32], line[:, 64:96])
        start = jnp.sum(jnp.where(doc_row == doc_number, begin, 0.0), axis=0, keepdims=True)
        starts.append(start)
        home_doc = home_doc + jnp.where(z_y == b, doc_row, 0)
        low = low + jnp.where(lane == b, start[:, 0:1], 0.0)
    diagonal = doc_number == lax.broadcasted_iota(jnp.int32, (32, 32), 1)
    home_doc = jnp.sum(jnp.where(diagonal, home_doc.astype(F32), 0.0), axis=1, keepdims=True)
    home_doc_ref[...] = jnp.broadcast_to(home_doc, (32, 128)).astype(jnp.int32)
    home_first = jnp.sum(jnp.where(lane == z_y, firsts, 0.0), axis=1, keepdims=True)
    home_pos_ref[...] = home_first + lax.broadcasted_iota(jnp.int32, (32, 128), 0).astype(F32)
    low = jnp.floor(low / STRIPE) * STRIPE
    need = jnp.where((base >= low) & (base <= firsts), 1.0, 0.0)
    below = lax.broadcasted_iota(jnp.int32, (64, 64), 1) <= lax.broadcasted_iota(jnp.int32, (64, 64), 0)
    rank = jnp.dot(
        jnp.where(below, 1.0, 0.0).astype(BF16), need.astype(BF16), preferred_element_type=F32
    )
    slot = (lane + 1).astype(F32)
    for b in range(8):
        chosen = (rank[:, b : b + 1] == slot) & (need[:, b : b + 1] > 0.0)
        row = jnp.sum(jnp.where(chosen, packed, 0.0), axis=0, keepdims=True)
        row = jnp.where(lane == 64, rank[63:64, b : b + 1], row)
        row = jnp.where(lane == 65, firsts[:, b : b + 1], row)
        row = jnp.concatenate([row[:, 0:96], starts[b]], axis=1)
        plan_ref[b : b + 1, :] = row.astype(jnp.int32)
    spot = lane.astype(F32)
    done, item = jnp.zeros((1, 1), F32), jnp.zeros((1, 128), F32)
    for b in range(8):
        after = done + jnp.floor((rank[63:64, b : b + 1] + (CHUNK - 1)) / CHUNK)
        item = item + jnp.where((spot >= done) & (spot < after), b * 16 + spot - done, 0.0)
        done = after
    item = jnp.where(spot >= done, 8.0 * 16, item)
    plan_ref[8:9, :] = item.astype(jnp.int32)
    plan_ref[9:10, :] = jnp.broadcast_to(done, (1, 128)).astype(jnp.int32)


PAIR = 4


def attend_kernel(heads, plan_rows_ref, left_ref, qd_hbm, *refs):
    kv_refs, out_hbm, plan_ref, qd_ref, kv_all, kv_now, acc_ref, top_ref, sum_ref, out_ref, sems, out_sems = (
        refs[:5],
        *refs[5:],
    )
    blocks, rows = qd_ref.shape[0:2]
    hd = 128
    width = heads * hd
    tall = rows * heads
    keys = CHUNK * STRIPE
    scale = 1.0 / math.sqrt(hd)

    copies = [
        pltpu.make_async_copy(plan_rows_ref, plan_ref, sems.at[5]),
        pltpu.make_async_copy(qd_hbm, qd_ref, sems.at[6]),
    ]
    row = 0
    for j, part in enumerate(kv_refs):
        copies.append(pltpu.make_async_copy(part, kv_all.at[pl.ds(row, part.shape[0])], sems.at[j]))
        row += part.shape[0]
    for copy in copies:
        copy.start()

    def clear(b, _):
        acc_ref[b] = jnp.zeros((tall, 3 * hd), F32)
        top_ref[b] = jnp.full((tall, 128), EMPTY, F32)
        sum_ref[b] = jnp.zeros((tall, 128), F32)
        return 0

    lax.fori_loop(0, blocks, clear, 0)
    for copy in copies:
        copy.wait()

    lane = lax.broadcasted_iota(jnp.int32, (1, keys), 1)
    diagonal = lax.broadcasted_iota(jnp.int32, (rows, rows), 0) == lax.broadcasted_iota(jnp.int32, (rows, rows), 1)
    row_i = lax.broadcasted_iota(jnp.int32, (rows, 1), 0)

    def wide(column):
        return jnp.broadcast_to(column, (tall, 128))

    def scores(i, item):
        held = item // 16
        c = item % 16
        b = jnp.minimum(held, blocks - 1)
        n = jnp.where(held < blocks, plan_ref[b, 64], 0)
        start = plan_rows_ref[pl.ds(b, 1), :][:, 96 : 96 + rows].astype(F32)
        start = jnp.sum(jnp.where(diagonal, start, 0.0), axis=1, keepdims=True).astype(jnp.int32)
        here = plan_ref[b, 65] + row_i
        key_pos = lane % STRIPE
        for u in range(CHUNK):
            slot = c * CHUNK + u
            valid = slot < n
            packed = plan_ref[b, jnp.minimum(slot, 63)]
            entry = jnp.where(valid, packed % 64, 0)
            base = jnp.where(valid, packed // 64, 1 << 24)
            kv_now[i, u * STRIPE : (u + 1) * STRIPE, :] = kv_all[pl.ds(pl.multiple_of(entry * STRIPE, STRIPE), STRIPE), :]
            key_pos = key_pos + jnp.where(lane // STRIPE == u, base, 0)
        bias = jnp.where((key_pos >= start) & (key_pos <= here), 0.0, MASKED).astype(F32)
        bias = jnp.concatenate([bias] * heads, axis=0)
        q, d = (
            jnp.concatenate(
                [qd_ref[b, :, side * width + h * hd : side * width + (h + 1) * hd] for h in range(heads)], axis=0
            )
            for side in range(2)
        )
        s = dot_t(q, kv_now[i, :, hd : 2 * hd]) * scale + bias
        return held, s, dot_t(d, kv_now[i, :, 0:hd])

    def softmax(held, s, dp):
        top = jnp.maximum(wide(jnp.max(s, axis=1, keepdims=True)), EMPTY).astype(BF16).astype(F32)
        p = jnp.exp(s - jnp.concatenate([top, top], axis=1))
        total = wide(jnp.sum(p, axis=1, keepdims=True))
        pb = p.astype(BF16)
        return held, top, total, pb, (pb.astype(F32) * dp).astype(BF16)

    def products(i, held, top, total, pb, w):
        attn = jnp.dot(pb, kv_now[i], preferred_element_type=F32)
        grad = jnp.dot(w, kv_now[i, :, hd : 2 * hd], preferred_element_type=F32)
        return held, top, total, (attn[:, 0:hd], attn[:, hd:], grad)

    def merge(held, top, total, sums):
        b = jnp.minimum(held, blocks)
        old = top_ref[b]
        new = jnp.maximum(old, top)
        keep, add = jnp.exp(old - new), jnp.exp(top - new)
        top_ref[b] = new
        sum_ref[b] = sum_ref[b] * keep + total * add
        for j, part in enumerate(sums):
            cols = slice(j * hd, (j + 1) * hd)
            acc_ref[b, :, cols] = acc_ref[b, :, cols] * keep + part * add

    def step(i, _):
        parts = [scores(j, plan_ref[8, i * PAIR + j]) for j in range(PAIR)]
        parts = [softmax(*part) for part in parts]
        parts = [products(j, *part) for j, part in enumerate(parts)]
        for part in parts:
            merge(*part)
        return 0

    lax.fori_loop(0, (plan_ref[9, 0] + PAIR - 1) // PAIR, step, 0)
    stat_lane = lax.broadcasted_iota(jnp.int32, (rows, 128), 1) - 64
    projected = []
    for h in range(heads):
        attn = acc_ref[0:blocks, h * rows : (h + 1) * rows, 0:hd].reshape(blocks * rows, hd).astype(BF16)
        projected.append(dot_t(attn, left_ref[:, h * hd : (h + 1) * hd].astype(BF16)))
    projected.append(jnp.zeros_like(projected[0]))
    for h in range(0, heads, 2):
        pair = jnp.concatenate(projected[h : h + 2], axis=1).astype(BF16)
        place = heads * 2 * hd + h // 2 * hd
        out_ref[:, :, place : place + hd] = pair.reshape(blocks, rows, hd)

    ones = jnp.ones((hd, 128), BF16)
    deltas = []
    for b in range(blocks):
        d = jnp.concatenate([qd_ref[b, :, width + h * hd : width + (h + 1) * hd] for h in range(heads)], axis=0)
        terms = d.astype(F32) * acc_ref[b, :, 0:hd]
        high = terms.astype(BF16)
        low = (terms - high.astype(F32)).astype(BF16)
        both = jnp.dot(jnp.concatenate([high, low], axis=0), ones, preferred_element_type=F32)
        deltas.append(both[0:tall] + both[tall:])
    for b in range(blocks):
        stats = jnp.zeros((rows, 128), F32)
        for h in range(heads):
            part = slice(h * rows, (h + 1) * rows)
            out_ref[b, :, h * 2 * hd : (h + 1) * 2 * hd] = acc_ref[b, part, hd:].astype(BF16)
            for place, value in enumerate((top_ref[b, part, :], sum_ref[b, part, :], deltas[b][part])):
                stats = jnp.where(stat_lane == place * STAT + h, value, stats)
        high = stats.astype(BF16)
        low = pltpu.roll(stats - high.astype(F32), 32, 1).astype(BF16)
        last = heads * 2 * hd + heads // 2 * hd
        out_ref[b, :, last : last + 128] = jnp.where(
            stat_lane < 0, out_ref[b, :, last : last + 128], jnp.where(stat_lane < 32, high, low)
        )
        pltpu.make_async_copy(out_ref.at[b], out_hbm.at[b], out_sems.at[b]).start()
    for b in range(blocks):
        pltpu.make_async_copy(out_ref.at[b], out_hbm.at[b], out_sems.at[b]).wait()


def combine_kernel(heads, part_ref, cos_ref, sin_ref, right_ref, grad_ref, tail_ref):
    blocks = part_ref.shape[0]
    hd = 128
    low_half = lax.broadcasted_iota(jnp.int32, (part_ref.shape[1], hd), 1) < 64
    stat = heads * 2 * hd + heads // 2 * hd + 64
    stats = [part_ref[r, :, stat - 64 : stat + 64].astype(F32) for r in range(blocks)]
    stats = [s[:, 64:96] + s[:, 96:128] for s in stats]
    field = lambda s, place: s[:, place * STAT : (place + 1) * STAT]
    tops = [field(s, 0) for s in stats]
    top = functools.reduce(jnp.maximum, tops)
    weights = [jnp.exp(t - top) for t in tops]
    total = sum(w * field(s, 1) for w, s in zip(weights, stats))
    total = jnp.where(lax.broadcasted_iota(jnp.int32, total.shape, 1) < heads, total, 1.0)
    weights = [w / total for w in weights]
    delta = sum(w * field(s, 2) for w, s in zip(weights, stats))
    scale = 1.0 / math.sqrt(hd)
    cos, sin = cos_ref[...], sin_ref[...]
    wide = [[jnp.broadcast_to(w[:, h : h + 1], (w.shape[0], hd)) for h in range(heads)] for w in weights]
    for h in range(heads):
        key_sum, grad_sum = (
            sum(
                wide[r][h] * part_ref[r, :, (2 * h + side) * hd : (2 * h + side + 1) * hd].astype(F32)
                for r in range(blocks)
            )
            for side in range(2)
        )
        raw = (grad_sum - delta[:, h : h + 1] * key_sum) * scale
        turned = jnp.concatenate([raw[:, hd // 2 :], raw[:, : hd // 2]], axis=1)
        grad_ref[:, h * hd : (h + 1) * hd] = (raw * cos + turned * sin).astype(BF16)
    tail_ref[:, 0:64] = dot_t(grad_ref[...], right_ref[...].astype(BF16))
    both = jnp.zeros((part_ref.shape[1], hd), F32)
    for r in range(blocks):
        for h in range(0, heads, 2):
            place = heads * 2 * hd + h // 2 * hd
            weight = jnp.where(low_half, wide[r][h], wide[r][h + 1] if h + 1 < heads else 0.0)
            both = both + weight * part_ref[r, :, place : place + hd].astype(F32)
    tail_ref[:, 64:128] = both[:, 0:64] + both[:, 64:128]


def docs_kernel(index_ref, head_ref, q_left_ref, o_right_ref, doc_ref, out_ref):
    h = index_ref[2]
    whole = head_ref[0] + head_ref[1] + head_ref[2] + head_ref[3]
    q_right, o_left_all = whole[:, 0:64], whole[:, 64:128]
    o_left = jnp.zeros((whole.shape[0], 16), F32)
    for k in range(4):
        o_left = o_left + jnp.where(h == k, o_left_all[:, 16 * k : 16 * k + 16], 0.0)
    doc = doc_ref[...]
    lane = lax.broadcasted_iota(jnp.int32, (whole.shape[0], 512), 1)
    mine = doc[:, 0:1] == lane // 16

    def split(value):
        high = value.astype(BF16)
        return high, (value - high.astype(F32)).astype(BF16)

    def outer(left, right):
        return lax.dot_general(left, right, (((0,), (0,)), ((), ())), preferred_element_type=F32)

    def terms(left, right):
        tiled = jnp.concatenate([left] * 8, axis=1)
        tiled = jnp.concatenate([tiled] * 4, axis=1)
        high, low = split(jnp.where(mine, tiled, 0.0))
        right_high, right_low = split(right)
        wide = outer(high, jnp.concatenate([right_high, right_low], axis=1))
        return wide[:, 0:64] + wide[:, 64:128] + outer(low, right_high)

    both = jnp.concatenate([terms(q_left_ref[...], q_right), terms(o_left, o_right_ref[...])], axis=1)
    out_ref[...] = both.reshape(out_ref.shape).astype(out_ref.dtype)


def total_kernel(part_ref, q_ref, o_ref):
    total = jnp.sum(part_ref[...].astype(F32), axis=0)
    for k in range(8):
        for side, ref in ((0, q_ref), (64, o_ref)):
            pair = [total[2 * k + j : 2 * k + j + 1, side : side + 64] for j in range(2)]
            ref[:, 128 * k : 128 * k + 128] = jnp.concatenate(pair, axis=1)


def call(kernel, out_shape, in_specs, out_specs, limit=LIMIT, **kw):
    return pl.pallas_call(
        kernel,
        out_shape=out_shape,
        in_specs=in_specs,
        out_specs=out_specs,
        compiler_params=pltpu.CompilerParams(vmem_limit_bytes=limit),
        **kw,
    )


def per_device(
    queries, keys, values, hidden_in, out_grad, w_out, q_left, q_right, o_left, o_right, positions, doc_ids
):
    shape = jax.ShapeDtypeStruct
    rows, width = queries.shape
    hd = keys.shape[1]
    heads = width // hd
    blocks = 8
    z, y, x, head = (lax.axis_index(a) for a in ("z", "y", "x", "head"))
    seq = (z * 2 + y) * 4 + x

    anywhere = pl.BlockSpec(memory_space=pl.ANY)
    index = call(
        place_kernel,
        shape((3,), jnp.int32),
        [SMEM],
        SMEM,
        cost_estimate=pl.CostEstimate(flops=40 << 30, bytes_accessed=64 << 20, transcendentals=0),
    )(jnp.stack([x, z * 2 + y, head]).astype(jnp.int32))
    kv = call(
        join_kernel,
        shape((keys.shape[0], 2 * hd), BF16),
        [SMEM] + [anywhere] * 2,
        anywhere,
        scratch_shapes=[pltpu.SemaphoreType.DMA((2,))],
        cost_estimate=pl.CostEstimate(flops=40 << 30, bytes_accessed=64 << 20, transcendentals=0),
    )(index, values, keys)
    kv_before = shifted(kv, "x", 1)
    kv_after = shifted(kv, "x", -1)
    half = shape((kv.shape[0] // 2, kv.shape[1]), BF16)
    anywhere = pl.BlockSpec(memory_space=pl.ANY)
    top, bottom = call(
        halves_kernel,
        (half, half),
        [anywhere] * 2,
        (anywhere, anywhere),
        scratch_shapes=[pltpu.SemaphoreType.DMA((2,))],
        cost_estimate=pl.CostEstimate(flops=40 << 30, bytes_accessed=64 << 20, transcendentals=0),
    )(kv_before, kv_after)
    far_top = shifted(top, "x", 1)
    far_bottom = shifted(bottom, "x", -1)

    hbm = pl.BlockSpec(memory_space=pltpu.HBM)
    attn_grad = dot_t(out_grad, w_out).astype(BF16)
    o_side = dot_t(out_grad, o_right)
    attn_grad, o_side = lax.optimization_barrier((attn_grad, o_side))
    mine = jnp.concatenate([queries, attn_grad], axis=1)
    qd = lax.all_to_all(jnp.broadcast_to(mine[None], (blocks,) + mine.shape), FAR, 0, 0)

    plan, home_doc, home_pos = call(
        plan_kernel,
        (shape((16, 128), jnp.int32), shape((rows, 128), jnp.int32), shape((rows, 128), F32)),
        [SMEM, hbm, hbm],
        (VMEM, VMEM, VMEM),
        scratch_shapes=[
            pltpu.VMEM(positions.shape, jnp.int32),
            pltpu.VMEM((256, 128), jnp.int32),
            pltpu.SemaphoreType.DMA((2,)),
        ],
    )(index, positions, doc_ids.reshape(256, 128))

    q_left_rows = lax.dynamic_slice_in_dim(q_left, head * 16, 16)
    q_side = dot_t(hidden_in, q_left_rows)

    out_lanes = heads * 2 * hd + (heads + 1) // 2 * hd
    tall = heads * rows
    parts = call(
        functools.partial(attend_kernel, heads),
        shape((blocks, rows, out_lanes), BF16),
        [VMEM] * 2 + [anywhere] * 6,
        anywhere,
        scratch_shapes=[
            pltpu.SMEM((16, 128), jnp.int32),
            pltpu.VMEM((blocks, rows, 2 * width), BF16),
            pltpu.VMEM((4096, 2 * hd), BF16),
            pltpu.VMEM((PAIR, CHUNK * STRIPE, 2 * hd), BF16),
            pltpu.VMEM((blocks + 1, tall, 3 * hd), F32),
            pltpu.VMEM((blocks + 1, tall, 128), F32),
            pltpu.VMEM((blocks + 1, tall, 128), F32),
            pltpu.VMEM((blocks, rows, out_lanes), BF16),
            pltpu.SemaphoreType.DMA((7,)),
            pltpu.SemaphoreType.DMA((blocks,)),
        ],
        limit=ATTEND_LIMIT,
    )(plan, o_left.astype(F32), qd, kv, kv_before, kv_after, far_top, far_bottom)
    parts = lax.all_to_all(parts, FAR, 0, 0)

    inverse_freq = ROPE_BASE ** (-(jnp.arange(hd // 2, dtype=F32) * 2.0) / hd)
    angles = home_pos * jnp.concatenate([inverse_freq, inverse_freq])[None, :]
    sign = jnp.where(jnp.arange(hd) < hd // 2, 1.0, -1.0).astype(F32)[None, :]
    query_grad, tail = call(
        functools.partial(combine_kernel, heads),
        (shape((rows, width), BF16), shape((rows, 128), F32)),
        [VMEM] * 4,
        (VMEM, VMEM),
    )(
        parts,
        jnp.cos(angles),
        jnp.sin(angles) * sign,
        q_right.astype(F32),
    )

    by_doc = call(
        docs_kernel,
        shape((32, 16, 128), BF16),
        [SMEM] + [VMEM] * 4,
        VMEM,
    )(index, lax.all_gather(tail, "head"), q_side, o_side, home_doc)
    by_doc = lax.all_to_all(by_doc, SEQ_AXES, 0, 0)
    q_docs, o_docs = call(
        total_kernel, (shape((1, 1024), F32), shape((1, 1024), F32)), [VMEM], (VMEM, VMEM)
    )(by_doc)
    return (query_grad, q_docs, o_docs)


def solution(mesh):
    grid = Mesh(mesh.devices.reshape(4, 2, 4, 4), ("z", "y", "x", "head"))
    both, seq, head = P(SEQ_AXES, "head"), P(SEQ_AXES, None), P("head", None)
    placed = (both, both, both, seq, seq, head, P(), P(None, "head"), P(None, "head"), P(), P(), P())
    return jax.shard_map(
        per_device, mesh=grid, in_specs=placed, out_specs=(both, both, both), check_vma=False
    )
```
